32 devices in a mesh: row: 8 (over z, core), col: 4 (over y, x).
Axes of the slice: x: 2, y: 2, z: 4, core: 2. Of those that a mesh axis runs over, the one named last changes fastest.
Arguments:
- inv_diag: bfloat16 [4, 8192, 8192], P(None, 'col', 'row'), as said below
- off_diag: bfloat16 [4, 1792, 8192], P(None, 'row', 'col'), may hold values from -0.0625 to 0.0625
- rhs: bfloat16 [4, 8192, 768], P(None, 'row'), may hold values from -6 to 6
- anc_rhs: float32 [1792, 768], P('row'), may hold values from -12 to 12
- dest_device: int32 [56, 4, 1], replicated, may hold values from 0 to 7, as said below
- dest_slot: int32 [56, 4], replicated, may hold values from 0 to 6
Outputs:
- solution: bfloat16 [4, 8192, 768], P(None, ('col', 'row'))
- anc_out: float32 [1792, 768], P('row')
The draws below stay inside these ranges and needn't reach their ends.
Inputs may be any that keep to these rules, and one draw needn't show every extreme that they name: inv_diag[s] is zero above its diagonal. Within one supernode s, distinct row blocks j belong to distinct ancestor blocks. Among the 28 entries dest_device[j, s] with j in one index of row's range of 7 blocks, every value occurs either 0 or exactly 7 times.
All inputs are finite; a program needn't handle non-finite values.
Results may differ from the reference program's by a relative error of at most 0.014.
Values may be sent and summed in bfloat16 or wider, within the bound.
No kernel may reach another device: no remote copies, remote signals or barrier semaphores. Data moves between devices by JAX's collectives and lax.ppermute only.
A program may use at most 128 MiB of HBM per device.

```python
import math
import jax
import jax.numpy as jnp
from jax import lax

SNODES = 4
WIDTH = 8192
NRHS = 768
BLOCK = 32
BLK_DEV = 7
ANC_DEV = 7
CAP = 7
BLOCKS = 56
OFF_ROWS = 1792
ANC_ROWS = 1792
N_ROW = 8
N_COL = 4


def draw_inv_diag(key, part):
    row_ids = jnp.arange(WIDTH, dtype=jnp.int32)[:, None]
    col_ids = jnp.arange(WIDTH, dtype=jnp.int32)[None, :]
    below = col_ids < row_ids
    on_diag = col_ids == row_ids

    def one_block(sub_key):
        key_off, key_diag = jax.random.split(sub_key)
        values = jax.random.normal(key_off, (WIDTH, WIDTH), jnp.float32)
        diag_values = jax.random.uniform(key_diag, (WIDTH, 1), jnp.float32, 0.5, 1.5)
        lower_part = jnp.where(below, values * (2.0 / math.sqrt(WIDTH)), 0.0)
        return (lower_part + jnp.where(on_diag, diag_values, 0.0)).astype(jnp.bfloat16)
    return lax.map(one_block, jax.random.split(key, SNODES))


def routing_tables(key):
    base_key = jax.random.fold_in(key, 7)
    key_order, key_shift, key_rows, key_slots = jax.random.split(base_key, 4)
    entries = SNODES * BLK_DEV
    owners_used = entries // CAP
    order = jax.random.permutation(key_order, entries).astype(jnp.int32).reshape(SNODES, BLK_DEV)
    shift_value = jax.random.randint(key_shift, (), 0, N_ROW, dtype=jnp.int32)
    offsets = (shift_value + order) % owners_used
    row_perm = jax.random.permutation(key_rows, N_ROW).astype(jnp.int32)
    row_inverse = jnp.argsort(row_perm, stable=True).astype(jnp.int32)
    source_rows = row_inverse[:, None, None]
    shifted = (source_rows + jnp.transpose(offsets, (1, 0))[None, :, :]) % N_ROW
    owner_table = row_perm[shifted]
    slot_perms = jax.vmap(lambda sub_key: jax.random.permutation(sub_key, BLK_DEV).astype(jnp.int32))(jax.random.split(key_slots, SNODES))
    slot_table = jnp.broadcast_to(jnp.transpose(slot_perms, (1, 0))[None, :, :], (N_ROW, BLK_DEV, SNODES))
    return (owner_table.reshape(N_ROW * BLK_DEV, SNODES).astype(jnp.int32), slot_table.reshape(N_ROW * BLK_DEV, SNODES).astype(jnp.int32))


def draw_dest_device(key, part):
    owner_table, slot_table = routing_tables(key)
    return owner_table[:, :, None]


def draw_dest_slot(key, part):
    owner_table, slot_table = routing_tables(key)
    return slot_table


def block_levels(key, shape, shards, smallest, top_value):
    level = 1.0
    for axis_at, blocks in shards:
        steps = jax.random.uniform(jax.random.fold_in(jax.random.fold_in(key, 6), axis_at), (blocks,), jnp.float32, smallest / len(shards), top_value / len(shards))
        level = level * jnp.repeat(jnp.exp(steps), shape[axis_at] // blocks).reshape((-1,) + (1,) * (len(shape) - 1 - axis_at))
    return level


def normal_values(own_key, shape, spread, limit, pieces=(), kind=jnp.bfloat16):
    result = spread * jax.random.normal(own_key, shape, jnp.float32)
    if pieces:
        result = result * block_levels(own_key, shape, pieces, -0.22, 0.18)
    return jnp.clip(result, -limit, limit).astype(kind)


def setup_inputs(seed: int = 0) -> dict:
    key_of = jax.random.split(jax.random.key(seed), 7)
    return {
        "inv_diag": draw_inv_diag(jax.random.fold_in(key_of[6], 71), 0),
        "off_diag": normal_values(key_of[1], (SNODES, OFF_ROWS, WIDTH), WIDTH ** -0.5, 0.0625, ((1, 8), (2, 4))),
        "rhs": normal_values(key_of[2], (SNODES, WIDTH, NRHS), 1.0, 6.0, ((1, 8),)),
        "anc_rhs": normal_values(key_of[3], (ANC_ROWS, NRHS), 2.0, 12.0, ((0, 8),), jnp.float32),
        "dest_device": draw_dest_device(jax.random.fold_in(key_of[6], 71), 0),
        "dest_slot": draw_dest_slot(jax.random.fold_in(key_of[6], 71), 0),
    }


def reference(inv_diag, off_diag, rhs, anc_rhs, dest_device, dest_slot):
    row_width = WIDTH // N_ROW
    col_width = WIDTH // N_COL

    def diag_step(running, group):
        factor_tile = lax.dynamic_slice_in_dim(inv_diag, group * row_width, row_width, 2).astype(jnp.float32)
        rhs_part = lax.dynamic_slice_in_dim(rhs, group * row_width, row_width, 1).astype(jnp.float32)
        term_value = jnp.einsum("swk,skn->swn", factor_tile, rhs_part)
        rounded = lax.optimization_barrier(term_value.astype(jnp.bfloat16))
        return running + rounded.astype(jnp.float32), None

    diag_total, _ = lax.scan(diag_step, jnp.zeros((SNODES, WIDTH, NRHS), jnp.float32), jnp.arange(N_ROW, dtype=jnp.int32))
    solution = diag_total.astype(jnp.bfloat16)

    def update_step(running, group):
        factor_tile = lax.dynamic_slice_in_dim(off_diag, group * col_width, col_width, 2).astype(jnp.float32)
        sol_part = lax.dynamic_slice_in_dim(solution, group * col_width, col_width, 1).astype(jnp.float32)
        term_value = jnp.einsum("srk,skn->srn", factor_tile, sol_part)
        rounded = lax.optimization_barrier(term_value.astype(jnp.bfloat16))
        return running + rounded.astype(jnp.float32), None

    update_total, _ = lax.scan(update_step, jnp.zeros((SNODES, OFF_ROWS, NRHS), jnp.float32), jnp.arange(N_COL, dtype=jnp.int32))
    update = update_total.astype(jnp.bfloat16)
    blocks = update.reshape(SNODES * BLOCKS, BLOCK * NRHS).astype(jnp.float32)
    target = (dest_device[:, :, 0] * ANC_DEV + dest_slot).astype(jnp.int32)
    target = jnp.transpose(target, (1, 0)).reshape(SNODES * BLOCKS)
    summed = jax.ops.segment_sum(blocks, target, num_segments=N_ROW * ANC_DEV)
    anc_out = anc_rhs - summed.reshape(ANC_ROWS, NRHS)
    return solution, anc_out
```

```python
import functools

import jax
import jax.numpy as jnp
from jax import lax
from jax.experimental import pallas as pl
from jax.experimental.pallas import tpu as pltpu
from jax.sharding import PartitionSpec as P

SNODES = 4
BLOCK = 32
CHUNK = 128
F32 = jnp.float32
BF16 = jnp.bfloat16


def add16(*terms):
    return functools.reduce(lambda a, b: a + b, [t.astype(F32) for t in terms]).astype(BF16)


def pick(array, index, axis):
    return lax.dynamic_index_in_dim(array, index, axis, keepdims=False)


def update_kernel(table_ref, place_ref, off_ref, *refs):
    pieces, out_ref, total = refs[:-2], refs[-2], refs[-1]
    nz = (len(pieces) + 1) // 2
    z = place_ref[0]
    blocks = off_ref.shape[2] // BLOCK
    total[...] = jnp.zeros_like(total)
    for s in range(SNODES):
        part = None
        for i, piece in enumerate(pieces):
            chip = jnp.clip(z + (i - nz + 1), 0, nz - 1)
            term = jnp.dot(off_ref[s, chip], piece[s], preferred_element_type=F32)
            part = term if part is None else part + term
        for b in range(blocks):
            a = table_ref[s * blocks + b]
            total[a] += part[b * BLOCK : (b + 1) * BLOCK]
    out_ref[...] = total[...].astype(out_ref.dtype)


def apply_update(table, place, off, pieces, anc_blocks):
    width = pieces[0].shape[2]
    flops = 2 * len(pieces) * off.shape[0] * off.shape[2] * off.shape[3] * width
    return pl.pallas_call(
        update_kernel,
        out_shape=jax.ShapeDtypeStruct((anc_blocks, BLOCK, width), BF16),
        in_specs=[pl.BlockSpec(memory_space=pltpu.SMEM)] * 2
        + [pl.BlockSpec(memory_space=pltpu.VMEM)] * (1 + len(pieces)),
        out_specs=pl.BlockSpec(memory_space=pltpu.VMEM),
        scratch_shapes=[pltpu.VMEM((anc_blocks, BLOCK, width), F32)],
        compiler_params=pltpu.CompilerParams(vmem_limit_bytes=40 * 1024 * 1024),
        cost_estimate=pl.CostEstimate(
            flops=flops, bytes_accessed=off.size * 2 + anc_blocks * BLOCK * width * 2, transcendentals=0
        ),
    )(table, place, off, *pieces)


def per_device(inv_diag, off_diag, rhs, anc_rhs, dest_device, dest_slot):
    n_row, n_col = lax.axis_size("row"), lax.axis_size("col")
    nz = n_row // 2
    row, col = lax.axis_index("row"), lax.axis_index("col")
    z, core = row // 2, row % 2
    own_rows = inv_diag.shape[1] // n_row
    anc_dev = anc_rhs.shape[0] // BLOCK
    anc_blocks = n_row * anc_dev
    nrhs = rhs.shape[2]
    pair = [(r, r ^ 1) for r in range(n_row)]

    def line(moves):
        return [(2 * i + q, 2 * j + q) for i, j in moves for q in range(2)]

    def right(chips):
        return line([(i, i + 1) for i in chips if i + 1 < nz])

    def left(chips):
        return line([(i, i - 1) for i in chips if i >= 1])

    per_dev = off_diag.shape[1] // BLOCK
    off = off_diag.reshape(SNODES, off_diag.shape[1], nz, 2, own_rows)
    mine = pick(off, core, 3).transpose(0, 2, 1, 3)
    theirs = lax.ppermute(pick(off, 1 - core, 3).transpose(0, 2, 1, 3), "row", pair)
    off = jnp.concatenate([mine, theirs], axis=2)
    target = (dest_device[:, :, 0] * anc_dev + dest_slot).reshape(n_row, per_dev, SNODES)
    table = jnp.concatenate([pick(target, row, 0), pick(target, row ^ 1, 0)], axis=0).T.reshape(-1)
    place = z.astype(jnp.int32).reshape(1)

    solutions, updates = [], []
    for at in range(0, nrhs, CHUNK):
        terms = jnp.einsum(
            "swk,skn->swn", inv_diag, rhs[:, :, at : at + CHUNK], preferred_element_type=F32
        ).astype(BF16)
        terms = terms.reshape(SNODES, nz, 2, own_rows, CHUNK)
        terms = add16(
            pick(terms, core, 2), lax.ppermute(pick(terms, 1 - core, 2), "row", pair)
        )
        from_left, from_right = [], []
        for t in range(1, nz):
            up = pick(terms, (z + nz - t) % nz, 1)
            from_left = [lax.ppermute(add16(up, *from_left), "row", right(range(t)))]
            down = pick(terms, (z + t) % nz, 1)
            from_right = [lax.ppermute(add16(down, *from_right), "row", left(range(nz - t, nz)))]
        own = add16(pick(terms, z, 1), *from_left, *from_right)
        solutions.append(own)
        lower, upper = [own], [own]
        for t in range(1, nz):
            lower.append(lax.ppermute(lower[-1], "row", right(range(t - 1, nz))))
            upper.append(lax.ppermute(upper[-1], "row", left(range(nz - t + 1))))
        pieces = lower[:0:-1] + [own] + upper[1:]
        total = apply_update(table, place, off, pieces, anc_blocks)
        total = total.reshape(nz, 2, anc_dev, n_col, BLOCK // n_col, CHUNK)
        total = add16(pick(total, core, 1), lax.ppermute(pick(total, 1 - core, 1), "row", pair))
        total = add16(
            pick(total, col, 2),
            *[
                lax.ppermute(pick(total, col ^ d, 2), "col", [(i, i ^ d) for i in range(n_col)])
                for d in range(1, n_col)
            ],
        )
        share = add16(
            pick(total, z, 0),
            *[
                lax.ppermute(
                    pick(total, (z + d) % nz, 0), "row", line([(i, (i + d) % nz) for i in range(nz)])
                )
                for d in range(1, nz)
            ],
        )
        whole = jnp.zeros((anc_dev, n_col) + share.shape[1:], BF16)
        whole = lax.dynamic_update_index_in_dim(whole, share, col, 1)
        for d in range(1, n_col):
            other = lax.ppermute(share, "col", [(i, i ^ d) for i in range(n_col)])
            whole = lax.dynamic_update_index_in_dim(whole, other, col ^ d, 1)
        updates.append(whole.reshape(anc_dev * BLOCK, CHUNK))
    solution = jnp.concatenate(solutions, axis=2)
    anc_out = anc_rhs - jnp.concatenate(updates, axis=1).astype(F32)
    return (solution, anc_out)


def solution(mesh):
    in_specs = (
        P(None, "col", "row"),
        P(None, "row", "col"),
        P(None, "row", None),
        P("row", None),
        P(),
        P(),
    )
    out_specs = (P(None, ("col", "row"), None), P("row", None))
    return jax.shard_map(
        per_device, mesh=mesh, in_specs=in_specs, out_specs=out_specs, check_vma=False
    )
```

```python
import functools

import jax
import jax.numpy as jnp
from jax import lax
from jax.experimental import pallas as pl
from jax.experimental.pallas import tpu as pltpu
from jax.sharding import PartitionSpec as P

SNODES = 4
BLOCK = 32
HALVES = 2
STREAMS = 2
F32 = jnp.float32
BF16 = jnp.bfloat16


def add16(*terms):
    return functools.reduce(lambda a, b: a + b, [t.astype(F32) for t in terms]).astype(BF16)


def pick(array, index, axis):
    return lax.dynamic_index_in_dim(array, index, axis, keepdims=False)


def after(value, *earlier):
    return lax.optimization_barrier((value,) + earlier)[0]


def update_kernel(table_ref, place_ref, off_ref, *refs):
    pieces, out_ref, total = refs[:-2], refs[-2], refs[-1]
    nz = off_ref.shape[1]
    z, core = place_ref[0], place_ref[1]
    step = 2 * core - 1
    blocks = off_ref.shape[3] // BLOCK
    per = SNODES // STREAMS
    total[...] = jnp.zeros_like(total)
    for s in range(SNODES):
        own = pieces[(s // per) * nz]
        part = jnp.dot(off_ref[s, z, core], own[s % per, core], preferred_element_type=F32)
        for t in range(1, nz):
            piece = pieces[(s // per) * nz + t]
            chip = jnp.clip(z + step * t, 0, nz - 1)
            for q in range(2):
                part += jnp.dot(off_ref[s, chip, q], piece[s % per, q], preferred_element_type=F32)
        for b in range(blocks):
            total[table_ref[s * blocks + b]] += part[b * BLOCK : (b + 1) * BLOCK]
    out_ref[...] = total[...].astype(out_ref.dtype)


def apply_update(table, place, off, pieces, anc_blocks):
    width = pieces[0].shape[-1]
    flops = 2 * off.size * width
    return pl.pallas_call(
        update_kernel,
        out_shape=jax.ShapeDtypeStruct((anc_blocks, BLOCK, width), BF16),
        in_specs=[pl.BlockSpec(memory_space=pltpu.SMEM)] * 2
        + [pl.BlockSpec(memory_space=pltpu.VMEM)] * (1 + len(pieces)),
        out_specs=pl.BlockSpec(memory_space=pltpu.VMEM),
        scratch_shapes=[pltpu.VMEM((anc_blocks, BLOCK, width), F32)],
        compiler_params=pltpu.CompilerParams(vmem_limit_bytes=48 * 1024 * 1024),
        cost_estimate=pl.CostEstimate(
            flops=flops, bytes_accessed=off.size * 2 + anc_blocks * BLOCK * width * 2, transcendentals=0
        ),
    )(table, place, off, *pieces)


def per_device(inv_diag, off_diag, rhs, anc_rhs, dest_device, dest_slot):
    n_row, n_col = lax.axis_size("row"), lax.axis_size("col")
    nz = n_row // 2
    row, col = lax.axis_index("row"), lax.axis_index("col")
    z, core = row // 2, row % 2
    side = 1 - 2 * core
    own_rows = inv_diag.shape[1] // n_row
    anc_dev = anc_rhs.shape[0] // BLOCK
    anc_blocks = n_row * anc_dev
    width = rhs.shape[2] // HALVES
    per = SNODES // STREAMS
    pair = [(r, r ^ 1) for r in range(n_row)]

    def hop(value, sources):
        up = [(2 * i, 2 * i + 2) for i in sources if i + 1 < nz]
        down = [(2 * (nz - 1 - i) + 1, 2 * (nz - 2 - i) + 1) for i in sources if i + 1 < nz]
        return lax.ppermute(value, "row", up + down)

    def product(s, n, *earlier):
        part = after(rhs[s * per : (s + 1) * per, :, n * width : (n + 1) * width], *earlier)
        terms = jnp.einsum(
            "swk,skn->swn", inv_diag[s * per : (s + 1) * per], part, preferred_element_type=F32
        ).astype(BF16)
        return terms.reshape(per, nz, 2, own_rows, width)

    def sum_cores(terms):
        away = jnp.stack([pick(terms, (z - side * j) % nz, 1) for j in range(1, nz)])
        other = lax.ppermute(away, "row", pair)
        return [pick(terms, z, 1)] + [
            add16(pick(terms, (z + side * j) % nz, 1), other[j - 1]) for j in range(1, nz)
        ]

    def share(total):
        total = total.reshape(nz, 2, anc_dev, n_col, BLOCK // n_col, width)
        total = add16(pick(total, core, 1), lax.ppermute(pick(total, 1 - core, 1), "row", pair))
        turns = [[(i, i ^ d) for i in range(n_col)] for d in range(1, n_col)]
        total = add16(
            pick(total, col, 2),
            *[lax.ppermute(pick(total, col ^ d, 2), "col", turns[d - 1]) for d in range(1, n_col)],
        )
        moves = [
            [(2 * i + q, 2 * ((i + d) % nz) + q) for i in range(nz) for q in range(2)] for d in range(1, nz)
        ]
        total = add16(
            pick(total, z, 0),
            *[lax.ppermute(pick(total, (z + d) % nz, 0), "row", moves[d - 1]) for d in range(1, nz)],
        )
        whole = jnp.zeros((anc_dev, n_col) + total.shape[1:], BF16)
        whole = lax.dynamic_update_index_in_dim(whole, total, col, 1)
        for d in range(1, n_col):
            other = lax.ppermute(total, "col", turns[d - 1])
            whole = lax.dynamic_update_index_in_dim(whole, other, col ^ d, 1)
        return whole.reshape(anc_dev * BLOCK, width)

    per_dev = off_diag.shape[1] // BLOCK
    target = (dest_device[:, :, 0] * anc_dev + dest_slot).reshape(n_row, per_dev, SNODES)
    table = jnp.concatenate([pick(target, row, 0), pick(target, row ^ 1, 0)], axis=0).T.reshape(-1)
    place = jnp.stack([z, core]).astype(jnp.int32)

    terms = [[None] * HALVES for _ in range(STREAMS)]
    last = ()
    for s in range(STREAMS):
        terms[s][0] = product(s, 0, *last)
        last = (terms[s][0],)
        terms[s][0] = sum_cores(terms[s][0])

    own = [[None] * HALVES for _ in range(STREAMS)]
    pieces = [[None] * HALVES for _ in range(STREAMS)]
    totals = []
    for s in range(STREAMS):
        flow = ()
        for t in range(1, nz):
            flow = (hop(add16(terms[s][0][nz - t], *flow), range(t)),)
            if t == 1:
                for n in range(1, HALVES):
                    terms[s][n] = sum_cores(product(s, n, flow[0]))
        for n in range(HALVES):
            mine = add16(terms[s][n][0], *flow)
            flow = ()
            own[s][n] = add16(mine, lax.ppermute(mine, "row", pair))
            got = [own[s][n]]
            for t in range(1, nz + 1):
                if t < nz:
                    got.append(hop(got[-1], range(t - 1, nz)))
                if t > 1 and n + 1 < HALVES:
                    send = add16(terms[s][n + 1][nz - t + 1], *flow)
                    if t == 2:
                        send = after(send, got[1])
                    flow = (hop(send, range(t - 1)),)
            pieces[s][n] = got
    off = off_diag.reshape(SNODES, off_diag.shape[1], nz, 2, own_rows).transpose(0, 2, 3, 1, 4)
    off = jnp.concatenate([off, lax.ppermute(after(off, terms[0][1][0]), "row", pair)], axis=3)
    for n in range(HALVES):
        flat = [p for s in range(STREAMS) for p in pieces[s][n]]
        totals.append(share(apply_update(table, place, off, flat, anc_blocks)))
    solution = jnp.concatenate(
        [jnp.concatenate([pick(own[s][n], core, 1) for n in range(HALVES)], axis=2) for s in range(STREAMS)],
        axis=0,
    )
    anc_out = anc_rhs - jnp.concatenate(totals, axis=1).astype(F32)
    return (solution, anc_out)


def solution(mesh):
    in_specs = (
        P(None, "col", "row"),
        P(None, "row", "col"),
        P(None, "row", None),
        P("row", None),
        P(),
        P(),
    )
    out_specs = (P(None, ("col", "row"), None), P("row", None))
    return jax.shard_map(
        per_device, mesh=mesh, in_specs=in_specs, out_specs=out_specs, check_vma=False
    )
```

```python
import functools

import jax
import jax.numpy as jnp
from jax import lax
from jax.experimental import pallas as pl
from jax.experimental.pallas import tpu as pltpu
from jax.sharding import PartitionSpec as P

SNODES = 4
BLOCK = 32
HALVES = 2
STREAMS = 2
F32 = jnp.float32
BF16 = jnp.bfloat16


def add16(*terms):
    return functools.reduce(lambda a, b: a + b, [t.astype(F32) for t in terms]).astype(BF16)


def pick(array, index, axis):
    return lax.dynamic_index_in_dim(array, index, axis, keepdims=False)


def after(value, *earlier):
    return lax.optimization_barrier((value,) + earlier)[0]


def product_kernel(meta_ref, tile_ref, rhs_ref, away_ref, keep_ref):
    terms = jnp.dot(tile_ref[0, 0], rhs_ref[0], preferred_element_type=F32).astype(BF16)
    is_away = pl.program_id(1) < meta_ref[2]

    @pl.when(is_away)
    def _():
        away_ref[0, 0] = terms

    @pl.when(jnp.logical_not(is_away))
    def _():
        keep_ref[0, 0] = terms


def apply_product(meta, tiles, rhs, first, per, n, width):
    nz, rows, depth = tiles.shape[1:]

    def tile_map(s, k, meta):
        j = k - meta[2]
        return first + s, meta[0] + meta[1] * jnp.where(j < 0, -1 - k, j), 0, 0

    def away_map(s, k, meta):
        return jnp.maximum(jnp.minimum(k, meta[2] - 1), 0), s, 0, 0

    def keep_map(s, k, meta):
        return jnp.maximum(k - meta[2], 0), s, 0, 0

    block = (1, 1, rows, width)
    return pl.pallas_call(
        product_kernel,
        grid_spec=pltpu.PrefetchScalarGridSpec(
            num_scalar_prefetch=1,
            grid=(per, nz),
            in_specs=[
                pl.BlockSpec((1, 1, rows, depth), tile_map),
                pl.BlockSpec((1, depth, width), lambda s, k, meta: (first + s, 0, n)),
            ],
            out_specs=[pl.BlockSpec(block, away_map), pl.BlockSpec(block, keep_map)],
        ),
        out_shape=[
            jax.ShapeDtypeStruct((nz - 1, per, rows, width), BF16),
            jax.ShapeDtypeStruct((nz, per, rows, width), BF16),
        ],
        compiler_params=pltpu.CompilerParams(vmem_limit_bytes=32 * 1024 * 1024),
        cost_estimate=pl.CostEstimate(
            flops=2 * per * nz * rows * depth * width,
            bytes_accessed=2 * per * (nz * rows * (depth + width) + depth * width),
            transcendentals=0,
        ),
    )(meta, tiles, rhs)


def update_kernel(table_ref, meta_ref, mine_ref, theirs_ref, *refs):
    pieces, out_ref, total = refs[:-2], refs[-2], refs[-1]
    per = pieces[0].shape[0]
    rows = pieces[0].shape[1]
    nz = len(pieces) * per // SNODES
    z, side = meta_ref[0], meta_ref[1]
    core = (1 - side) // 2
    height = mine_ref.shape[-2]
    blocks = 2 * height // BLOCK

    def factor(s, start, count):
        if len(mine_ref.shape) == 3:
            at = pl.ds(pl.multiple_of(start * count, count), count)
            return jnp.concatenate([mine_ref[s, :, at], theirs_ref[s, :, at]], axis=0)
        per_index = rows // count
        both = jnp.concatenate([mine_ref[s, start // per_index], theirs_ref[s, start // per_index]], axis=0)
        if per_index == 1:
            return both
        return jnp.where(core == 0, both[:, :count], both[:, count:])

    total[...] = jnp.zeros_like(total)
    half = rows // 2
    for s in range(SNODES):
        own = pieces[(s // per) * nz]
        part = jnp.dot(
            factor(s, 2 * z + core, half),
            own[s % per, pl.ds(pl.multiple_of(core * half, half), half)],
            preferred_element_type=F32,
        )
        for t in range(1, nz):
            chip = jnp.clip(z - side * t, 0, nz - 1)
            part += jnp.dot(
                factor(s, chip, rows), pieces[(s // per) * nz + t][s % per], preferred_element_type=F32
            )
        for b in range(blocks):
            total[table_ref[s * blocks + b]] += part[b * BLOCK : (b + 1) * BLOCK]
    out_ref[...] = total[...].astype(out_ref.dtype)


def apply_update(table, meta, mine, theirs, pieces, anc_blocks):
    width = pieces[0].shape[-1]
    return pl.pallas_call(
        update_kernel,
        out_shape=jax.ShapeDtypeStruct((anc_blocks, BLOCK, width), BF16),
        in_specs=[pl.BlockSpec(memory_space=pltpu.SMEM)] * 2
        + [pl.BlockSpec(memory_space=pltpu.VMEM)] * (2 + len(pieces)),
        out_specs=pl.BlockSpec(memory_space=pltpu.VMEM),
        scratch_shapes=[pltpu.VMEM((anc_blocks, BLOCK, width), F32)],
        compiler_params=pltpu.CompilerParams(vmem_limit_bytes=48 * 1024 * 1024),
        cost_estimate=pl.CostEstimate(
            flops=4 * mine.size * width,
            bytes_accessed=mine.size * 4 + anc_blocks * BLOCK * width * 2,
            transcendentals=0,
        ),
    )(table, meta, mine, theirs, *pieces)


def per_device(inv_diag, off_diag, rhs, anc_rhs, dest_device, dest_slot):
    n_row, n_col = lax.axis_size("row"), lax.axis_size("col")
    nz = n_row // 2
    row, col = lax.axis_index("row"), lax.axis_index("col")
    z, core = row // 2, row % 2
    side = 1 - 2 * core
    own_rows = inv_diag.shape[1] // n_row
    anc_dev = anc_rhs.shape[0] // BLOCK
    anc_blocks = n_row * anc_dev
    width = rhs.shape[2] // HALVES
    per = SNODES // STREAMS
    pair = [(r, r ^ 1) for r in range(n_row)]

    def hop(value, sources):
        up = [(2 * i, 2 * i + 2) for i in sources if i + 1 < nz]
        down = [(2 * (nz - 1 - i) + 1, 2 * (nz - 2 - i) + 1) for i in sources if i + 1 < nz]
        return lax.ppermute(value, "row", up + down)

    tiles = inv_diag.reshape(SNODES, nz, 2 * own_rows, inv_diag.shape[2])
    meta = jnp.stack([z, side, jnp.where(core == 0, z, nz - 1 - z)]).astype(jnp.int32)

    def product(s, n, *earlier):
        return apply_product(after(meta, *earlier), tiles, rhs, s * per, per, n, width)

    def sum_cores(terms):
        away, keep = terms
        other = lax.ppermute(away, "row", pair)
        return [(keep[0],)] + [(keep[j], other[j - 1]) for j in range(1, nz)]

    turns = [[(i, i ^ d) for i in range(n_col)] for d in range(1, n_col)]
    moves = [[(2 * i + q, 2 * ((i + d) % nz) + q) for i in range(nz) for q in range(2)] for d in range(1, nz)]

    def share_cores(total):
        total = total.reshape(nz, 2, anc_dev, n_col, BLOCK // n_col, width)
        return add16(pick(total, core, 1), lax.ppermute(pick(total, 1 - core, 1), "row", pair))

    def share_col(total):
        return add16(
            pick(total, col, 2),
            *[lax.ppermute(pick(total, col ^ d, 2), "col", turns[d - 1]) for d in range(1, n_col)],
        )

    def share_line(total):
        return add16(
            pick(total, z, 0),
            *[lax.ppermute(pick(total, (z + d) % nz, 0), "row", moves[d - 1]) for d in range(1, nz)],
        )

    def share_out(total):
        whole = jnp.zeros((anc_dev, n_col) + total.shape[1:], BF16)
        whole = lax.dynamic_update_index_in_dim(whole, total, col, 1)
        for d in range(1, n_col):
            other = lax.ppermute(total, "col", turns[d - 1])
            whole = lax.dynamic_update_index_in_dim(whole, other, col ^ d, 1)
        return whole.reshape(anc_dev * BLOCK, width)

    shares = [share_cores, share_col, share_line, share_out]

    per_dev = off_diag.shape[1] // BLOCK
    target = (dest_device[:, :, 0] * anc_dev + dest_slot).reshape(n_row, per_dev, SNODES)
    table = jnp.concatenate([pick(target, row, 0), pick(target, row ^ 1, 0)], axis=0).T.reshape(-1)
    split = (lambda x: x) if (own_rows % 128 == 0) else (
        lambda x: x.reshape(SNODES, x.shape[1], nz, 2 * own_rows).transpose(0, 2, 1, 3)
    )

    terms = [[None] * HALVES for _ in range(STREAMS)]
    for s in range(STREAMS):
        terms[s][0] = product(s, 0, *(terms[s - 1][0] if s else ()))
    for s in range(STREAMS):
        terms[s][0] = sum_cores(terms[s][0])

    own = [[None] * HALVES for _ in range(STREAMS)]
    pieces = [[None] * HALVES for _ in range(STREAMS)]
    flows = [()] * STREAMS
    for t in range(1, nz):
        for s in range(STREAMS):
            flows[s] = (hop(add16(*terms[s][0][nz - t], *flows[s]), range(t)),)
            if t == 1:
                for n in range(1, HALVES):
                    terms[s][n] = sum_cores(product(s, n, flows[s][0]))
        if t == nz - 1:
            theirs = lax.ppermute(after(off_diag, flows[0][0]), "row", pair)
    mine, theirs = split(off_diag), split(theirs)

    total, totals = None, []
    for n in range(HALVES):
        partial = [add16(*terms[s][n][0], *flows[s]) for s in range(STREAMS)]
        if total is not None:
            partial[0] = after(partial[0], total)
        for s in range(STREAMS):
            own[s][n] = add16(partial[s], lax.ppermute(partial[s], "row", pair))
        flows = [()] * STREAMS
        got = [[own[s][n]] for s in range(STREAMS)]
        for t in range(1, nz + 1):
            for s in range(STREAMS):
                if t < nz:
                    send = got[s][-1]
                    if total is not None and s == 0 and t <= len(shares):
                        total = shares[t - 1](total)
                        send = after(send, total) if t > 1 else send
                    got[s].append(hop(send, range(t - 1, nz)))
                if t > 1 and n + 1 < HALVES:
                    send = add16(*terms[s][n + 1][nz - t + 1], *flows[s])
                    if t == 2:
                        send = after(send, got[s][1])
                    flows[s] = (hop(send, range(t - 1)),)
        if total is not None:
            for stage in shares[nz - 1 :]:
                total = stage(total)
            totals.append(total)
        flat = [p for s in range(STREAMS) for p in got[s]]
        total = apply_update(table, meta, mine, theirs, flat, anc_blocks)
    for stage in shares:
        total = stage(total)
    totals.append(total)
    solution = jnp.concatenate(
        [jnp.concatenate(
                [lax.dynamic_slice_in_dim(own[s][n], core * own_rows, own_rows, 1) for n in range(HALVES)], axis=2
            ) for s in range(STREAMS)],
        axis=0,
    )
    anc_out = anc_rhs - jnp.concatenate(totals, axis=1).astype(F32)
    return (solution, anc_out)


def solution(mesh):
    in_specs = (
        P(None, "col", "row"),
        P(None, "row", "col"),
        P(None, "row", None),
        P("row", None),
        P(),
        P(),
    )
    out_specs = (P(None, ("col", "row"), None), P("row", None))
    return jax.shard_map(
        per_device, mesh=mesh, in_specs=in_specs, out_specs=out_specs, check_vma=False
    )
```

```python
import functools

import jax
import jax.numpy as jnp
from jax import lax
from jax.experimental import pallas as pl
from jax.experimental.pallas import tpu as pltpu
from jax.sharding import PartitionSpec as P

SNODES = 4
BLOCK = 32
HALVES = 2
AHEAD = 4
STREAMS = 2
F32 = jnp.float32
BF16 = jnp.bfloat16


def add16(*terms):
    return functools.reduce(lambda a, b: a + b, [t.astype(F32) for t in terms]).astype(BF16)


def pick(array, index, axis):
    return lax.dynamic_index_in_dim(array, index, axis, keepdims=False)


def after(value, *earlier):
    return lax.optimization_barrier((value,) + earlier)[0]


def product_kernel(first, meta_ref, tile_ref, rhs_ref, *refs):
    outs, (tile, part, terms, tile_sem, part_sem, out_sem) = refs[:-6], refs[-6:]
    per, nz = tile.shape[:2]
    z, side = meta_ref[0], meta_ref[1]
    width = terms.shape[-1]
    reads = []
    for s in range(per):
        reads.append([pltpu.make_async_copy(rhs_ref.at[first + s], part.at[s], part_sem.at[s])])
        for d in range(nz):
            reads[s].append(pltpu.make_async_copy(tile_ref.at[first + s, d], tile.at[s, d], tile_sem.at[s, d]))
    queue = [copy for copies in reads for copy in copies]
    for copy in queue[:AHEAD]:
        copy.start()
    queue = queue[AHEAD:]

    def await_next(copy):
        copy.wait()
        if queue:
            queue.pop(0).start()

    writes = []
    for s in range(per):
        await_next(reads[s][0])
        for d in range(nz):
            await_next(reads[s][d + 1])
            both = jnp.dot(tile[s, d], part[s], preferred_element_type=F32).astype(BF16)
            place = (d - z) * side
            for n in range(HALVES):
                terms[s, d, n] = both[:, n * width : (n + 1) * width]
                source, sem = terms.at[s, d, n], out_sem.at[s, d, n]
                away = pltpu.make_async_copy(source, outs[2 * n].at[jnp.clip(-1 - place, 0, nz - 2), s], sem)
                keep = pltpu.make_async_copy(source, outs[2 * n + 1].at[jnp.clip(place, 0, nz - 1), s], sem)
                pl.when(place < 0)(away.start)
                pl.when(place >= 0)(keep.start)
                writes.append((place, away, keep))
    for place, away, keep in writes:
        pl.when(place < 0)(away.wait)
        pl.when(place >= 0)(keep.wait)


def apply_product(meta, tiles, rhs, first, per):
    nz, rows, depth = tiles.shape[1:]
    width = rhs.shape[2] // HALVES
    hbm = pl.BlockSpec(memory_space=pl.ANY)
    outs = pl.pallas_call(
        functools.partial(product_kernel, first),
        in_specs=[pl.BlockSpec(memory_space=pltpu.SMEM), hbm, hbm],
        out_specs=[hbm] * (2 * HALVES),
        out_shape=[
            jax.ShapeDtypeStruct((nz - 1, per, rows, width), BF16),
            jax.ShapeDtypeStruct((nz, per, rows, width), BF16),
        ]
        * HALVES,
        scratch_shapes=[
            pltpu.VMEM((per, nz, rows, depth), BF16),
            pltpu.VMEM((per, depth, rhs.shape[2]), BF16),
            pltpu.VMEM((per, nz, HALVES, rows, width), BF16),
            pltpu.SemaphoreType.DMA((per, nz)),
            pltpu.SemaphoreType.DMA((per,)),
            pltpu.SemaphoreType.DMA((per, nz, HALVES)),
        ],
        compiler_params=pltpu.CompilerParams(vmem_limit_bytes=56 * 1024 * 1024),
        cost_estimate=pl.CostEstimate(
            flops=2 * per * nz * rows * depth * rhs.shape[2],
            bytes_accessed=2 * per * (nz * rows * (depth + rhs.shape[2]) + depth * rhs.shape[2]),
            transcendentals=0,
        ),
    )(meta, tiles, rhs)
    return [outs[2 * n : 2 * n + 2] for n in range(HALVES)]


def update_kernel(places, has_base, table_ref, meta_ref, mine_ref, theirs_ref, *refs):
    sources, scratch = refs[has_base : 2 * len(places) + has_base], refs[2 * len(places) + has_base :]
    out_ref, total, part, rows_both, pieces, sem, piece_sem = scratch[:7]
    per, rows = sources[0].shape[:2]
    z, side, last = meta_ref[0], meta_ref[1], meta_ref[2]
    core = (1 - side) // 2
    upstream = jnp.where(core == 0, z, last - z)
    height = part.shape[0] // 2
    blocks = 2 * height // BLOCK
    half = rows // 2
    raw = len(mine_ref.shape) == 3
    only = places[0] if len(places) == 1 else None
    reach = upstream >= places[0]
    if has_base:
        base = pltpu.make_async_copy(refs[0], scratch[7], scratch[8])
        base.start()
    reads, arrive = [], []
    for s in range(SNODES):
        for i, ref in enumerate((mine_ref, theirs_ref)):
            chip = jnp.clip(z - side * places[0], 0, last)
            if only is not None and raw:
                source = ref.at[s, :, pl.ds(pl.multiple_of(chip * rows, rows), rows)]
                spot = rows_both.at[s, pl.ds(i * height, height), pl.ds(0, rows)]
            elif raw:
                source, spot = ref.at[s], rows_both.at[s, pl.ds(i * height, height)]
            else:
                source, spot = ref.at[s], rows_both.at[s, :, pl.ds(i * height, height)]
            reads.append(pltpu.make_async_copy(source, spot, sem.at[s, i]))
            pl.when(reach)(reads[-1].start)
        if s % per == 0:
            for i, t in enumerate(places):
                k = (s // per) * len(places) + i
                arrive.append(pltpu.make_async_copy(sources[k], pieces.at[k], piece_sem.at[k]))
                pl.when(upstream >= t)(arrive[-1].start)

    def factor(s, start, count):
        if only is not None and raw:
            return rows_both[s, :, :rows]
        if raw:
            return rows_both[s, :, pl.ds(pl.multiple_of(start * count, count), count)]
        both = rows_both[s, start // (rows // count)]
        return both if count == rows else jnp.where(core == 0, both[:, :count], both[:, count:])

    if has_base:
        base.wait()
        total[...] = scratch[7][...].astype(F32)
    else:
        total[...] = jnp.zeros_like(total)

    @pl.when(reach)
    def _():
        for s in range(SNODES):
            reads[2 * s].wait()
            reads[2 * s + 1].wait()
            first = (s // per) * len(places)
            if s % per == 0:
                for i, t in enumerate(places):
                    pl.when(upstream >= t)(arrive[first + i].wait)
            for i, t in enumerate(places):
                if t == 0:
                    part[...] = jnp.dot(
                        factor(s, 2 * z + core, half),
                        pieces[first, s % per, pl.ds(pl.multiple_of(core * half, half), half)],
                        preferred_element_type=F32,
                    )
                    continue
                chip = jnp.clip(z - side * t, 0, last)
                if i == 0:
                    part[...] = jnp.dot(
                        factor(s, chip, rows), pieces[first, s % per], preferred_element_type=F32
                    )
                    continue

                @pl.when(upstream >= t)
                def _():
                    part[...] += jnp.dot(
                        factor(s, chip, rows), pieces[first + i, s % per], preferred_element_type=F32
                    )

            for b in range(blocks):
                total[table_ref[s * blocks + b]] += part[b * BLOCK : (b + 1) * BLOCK]

    out_ref[...] = total[...].astype(out_ref.dtype)


def apply_update(table, meta, mine, theirs, got, places, anc_blocks, base=None):
    pieces = [x[t] for x in got for t in places]
    width = pieces[0].shape[-1]
    height = mine.shape[-2]
    hbm = pl.BlockSpec(memory_space=pl.ANY)
    both = list(mine.shape)
    both[-2] *= 2
    if mine.ndim == 3 and len(places) == 1:
        both[-1] = pieces[0].shape[-2]
    block = (anc_blocks, BLOCK, width)
    has_base = base is not None
    return pl.pallas_call(
        functools.partial(update_kernel, places, has_base),
        out_shape=jax.ShapeDtypeStruct(block, BF16),
        in_specs=[pl.BlockSpec(memory_space=pltpu.SMEM)] * 2 + [hbm] * (2 + has_base + len(pieces)),
        out_specs=pl.BlockSpec(memory_space=pltpu.VMEM),
        scratch_shapes=[
            pltpu.VMEM(block, F32),
            pltpu.VMEM((2 * height, width), F32),
            pltpu.VMEM(tuple(both), BF16),
            pltpu.VMEM((len(pieces),) + pieces[0].shape, BF16),
            pltpu.SemaphoreType.DMA((SNODES, 2)),
            pltpu.SemaphoreType.DMA((len(pieces),)),
        ]
        + [pltpu.VMEM(block, BF16), pltpu.SemaphoreType.DMA] * has_base,
        compiler_params=pltpu.CompilerParams(vmem_limit_bytes=40 * 1024 * 1024),
        cost_estimate=pl.CostEstimate(
            flops=4 * mine.size * width * len(places) // len(got[0]),
            bytes_accessed=mine.size * 4 + anc_blocks * BLOCK * width * 2,
            transcendentals=0,
        ),
    )(table, meta, mine, theirs, *([base] if has_base else []), *pieces)


def per_device(inv_diag, off_diag, rhs, anc_rhs, dest_device, dest_slot):
    n_row, n_col = lax.axis_size("row"), lax.axis_size("col")
    nz = n_row // 2
    row, col = lax.axis_index("row"), lax.axis_index("col")
    z, core = row // 2, row % 2
    side = 1 - 2 * core
    own_rows = inv_diag.shape[1] // n_row
    anc_dev = anc_rhs.shape[0] // BLOCK
    anc_blocks = n_row * anc_dev
    width = rhs.shape[2] // HALVES
    per = SNODES // STREAMS
    pair = [(r, r ^ 1) for r in range(n_row)]

    def hop(value, sources):
        up = [(2 * i, 2 * i + 2) for i in sources if i + 1 < nz]
        down = [(2 * (nz - 1 - i) + 1, 2 * (nz - 2 - i) + 1) for i in sources if i + 1 < nz]
        return lax.ppermute(value, "row", up + down)

    tiles = inv_diag.reshape(SNODES, nz, 2 * own_rows, inv_diag.shape[2])
    meta = jnp.stack([z, side, jnp.full_like(z, nz - 1)]).astype(jnp.int32)

    def sum_cores(terms):
        away, keep = terms
        other = lax.ppermute(away, "row", pair)
        return [(keep[0],)] + [(keep[j], other[j - 1]) for j in range(1, nz)]

    turns = [[(i, i ^ d) for i in range(n_col)] for d in range(1, n_col)]
    moves = [[(2 * i + q, 2 * ((i + d) % nz) + q) for i in range(nz) for q in range(2)] for d in range(1, nz)]

    def share_cores(total):
        total = total.reshape(nz, 2, anc_dev, n_col, BLOCK // n_col, width)
        return add16(pick(total, core, 1), lax.ppermute(pick(total, 1 - core, 1), "row", pair))

    def share_col(total):
        return add16(
            pick(total, col, 2),
            *[lax.ppermute(pick(total, col ^ d, 2), "col", turns[d - 1]) for d in range(1, n_col)],
        )

    def share_line(total):
        return add16(
            pick(total, z, 0),
            *[lax.ppermute(pick(total, (z + d) % nz, 0), "row", moves[d - 1]) for d in range(1, nz)],
        )

    def share_out(total):
        whole = jnp.zeros((anc_dev, n_col) + total.shape[1:], BF16)
        whole = lax.dynamic_update_index_in_dim(whole, total, col, 1)
        for d in range(1, n_col):
            other = lax.ppermute(total, "col", turns[d - 1])
            whole = lax.dynamic_update_index_in_dim(whole, other, col ^ d, 1)
        return whole.reshape(anc_dev * BLOCK, whole.shape[-1])

    shares = [share_cores, share_col, share_line]

    per_dev = off_diag.shape[1] // BLOCK
    target = (dest_device[:, :, 0] * anc_dev + dest_slot).reshape(n_row, per_dev, SNODES)
    table = jnp.concatenate([pick(target, row, 0), pick(target, row ^ 1, 0)], axis=0).T.reshape(-1)
    split = (lambda x: x) if (own_rows % 128 == 0) else (
        lambda x: x.reshape(SNODES, x.shape[1], nz, 2 * own_rows).transpose(0, 2, 1, 3)
    )

    terms, last = [], ()
    for s in range(STREAMS):
        raw = apply_product(after(meta, *last), tiles, rhs, s * per, per)
        last = (raw[0][1],)
        terms.append([sum_cores(x) for x in raw])

    own = [[None] * HALVES for _ in range(STREAMS)]
    upstream = jnp.where(core == 0, z, nz - 1 - z)
    flows = [()] * STREAMS
    for t in range(1, nz):
        for s in range(STREAMS):
            flows[s] = (hop(add16(*terms[s][0][nz - t], *flows[s]), range(t)),)
        if t == 1:
            theirs = lax.ppermute(after(off_diag, flows[0][0]), "row", pair)
    mine, theirs = split(off_diag), split(theirs)

    waiting = None
    for n in range(HALVES):
        partial = [add16(*terms[s][n][0], *flows[s]) for s in range(STREAMS)]
        for s in range(STREAMS):
            own[s][n] = add16(partial[s], lax.ppermute(partial[s], "row", pair))
        got = [[own[s][n]] for s in range(STREAMS)]
        for t in range(1, nz + 1):
            for s in range(STREAMS):
                send = got[s][-1]
                if n + 1 < HALVES:
                    if t > 1:
                        late = functools.reduce(
                            lambda a, b: a + b, [x.astype(F32) for x in terms[s][n + 1][nz - t + 1]]
                        )
                        send = (send.astype(F32) + jnp.where(upstream >= t - 1, 0.0, late)).astype(BF16)
                    got[s].append(hop(send, range(nz)))
                elif t < nz:
                    if n and s == STREAMS - 1 and t == nz - 1:
                        total = share_cores(total)
                        send = after(send, total)
                    got[s].append(hop(send, range(t - 1, nz)))
                    if n and s == 0 and t == 1:
                        total = apply_update(
                            table, after(meta, got[0][1]), mine, theirs, before, range(nz), anc_blocks
                        )
        if n + 1 < HALVES:
            flows = [(got[s].pop(),) for s in range(STREAMS)]
        if n:
            waiting = share_col(total)
        before = got
    total = apply_update(table, after(meta, got[0][nz - 1]), mine, theirs, got, range(nz - 1), anc_blocks)
    total = apply_update(table, after(meta, waiting), mine, theirs, got, [nz - 1], anc_blocks, total)
    total = jnp.concatenate([waiting, share_col(share_cores(total))], axis=-1)
    update = share_out(share_line(total))
    solution = jnp.concatenate(
        [jnp.concatenate(
                [lax.dynamic_slice_in_dim(own[s][n], core * own_rows, own_rows, 1) for n in range(HALVES)], axis=2
            ) for s in range(STREAMS)],
        axis=0,
    )
    anc_out = anc_rhs - update.astype(F32)
    return (solution, anc_out)


def solution(mesh):
    in_specs = (
        P(None, "col", "row"),
        P(None, "row", "col"),
        P(None, "row", None),
        P("row", None),
        P(),
        P(),
    )
    out_specs = (P(None, ("col", "row"), None), P("row", None))
    return jax.shard_map(
        per_device, mesh=mesh, in_specs=in_specs, out_specs=out_specs, check_vma=False
    )
```

```python
import functools

import jax
import jax.numpy as jnp
from jax import lax
from jax.experimental import pallas as pl
from jax.experimental.pallas import tpu as pltpu
from jax.sharding import PartitionSpec as P

SNODES = 4
BLOCK = 32
HALVES = 2
AHEAD = 4
STREAMS = 2
F32 = jnp.float32
BF16 = jnp.bfloat16


def add16(*terms):
    return functools.reduce(lambda a, b: a + b, [t.astype(F32) for t in terms]).astype(BF16)


def pick(array, index, axis):
    return lax.dynamic_index_in_dim(array, index, axis, keepdims=False)


def after(value, *earlier):
    return lax.optimization_barrier((value,) + earlier)[0]


def product_kernel(first, meta_ref, tile_ref, rhs_ref, *refs):
    outs, (tile, part, terms, tile_sem, part_sem, out_sem) = refs[:-6], refs[-6:]
    per, nz = tile.shape[:2]
    z, side = meta_ref[0], meta_ref[1]
    width = terms.shape[-1]
    reads = []
    for s in range(per):
        reads.append([pltpu.make_async_copy(rhs_ref.at[first + s], part.at[s], part_sem.at[s])])
        for d in range(nz):
            reads[s].append(pltpu.make_async_copy(tile_ref.at[first + s, d], tile.at[s, d], tile_sem.at[s, d]))
    queue = [copy for copies in reads for copy in copies]
    for copy in queue[:AHEAD]:
        copy.start()
    queue = queue[AHEAD:]

    def await_next(copy):
        copy.wait()
        if queue:
            queue.pop(0).start()

    writes = []
    for s in range(per):
        await_next(reads[s][0])
        for d in range(nz):
            await_next(reads[s][d + 1])
            both = jnp.dot(tile[s, d], part[s], preferred_element_type=F32).astype(BF16)
            place = (d - z) * side
            for n in range(HALVES):
                terms[s, d, n] = both[:, n * width : (n + 1) * width]
                source, sem = terms.at[s, d, n], out_sem.at[s, d, n]
                away = pltpu.make_async_copy(source, outs[2 * n].at[jnp.clip(-1 - place, 0, nz - 2), s], sem)
                keep = pltpu.make_async_copy(source, outs[2 * n + 1].at[jnp.clip(place, 0, nz - 1), s], sem)
                pl.when(place < 0)(away.start)
                pl.when(place >= 0)(keep.start)
                writes.append((place, away, keep))
    for place, away, keep in writes:
        pl.when(place < 0)(away.wait)
        pl.when(place >= 0)(keep.wait)


def apply_product(meta, tiles, rhs, first, per):
    nz, rows, depth = tiles.shape[1:]
    width = rhs.shape[2] // HALVES
    hbm = pl.BlockSpec(memory_space=pl.ANY)
    outs = pl.pallas_call(
        functools.partial(product_kernel, first),
        in_specs=[pl.BlockSpec(memory_space=pltpu.SMEM), hbm, hbm],
        out_specs=[hbm] * (2 * HALVES),
        out_shape=[
            jax.ShapeDtypeStruct((nz - 1, per, rows, width), BF16),
            jax.ShapeDtypeStruct((nz, per, rows, width), BF16),
        ]
        * HALVES,
        scratch_shapes=[
            pltpu.VMEM((per, nz, rows, depth), BF16),
            pltpu.VMEM((per, depth, rhs.shape[2]), BF16),
            pltpu.VMEM((per, nz, HALVES, rows, width), BF16),
            pltpu.SemaphoreType.DMA((per, nz)),
            pltpu.SemaphoreType.DMA((per,)),
            pltpu.SemaphoreType.DMA((per, nz, HALVES)),
        ],
        compiler_params=pltpu.CompilerParams(vmem_limit_bytes=56 * 1024 * 1024),
        cost_estimate=pl.CostEstimate(
            flops=2 * per * nz * rows * depth * rhs.shape[2],
            bytes_accessed=2 * per * (nz * rows * (depth + rhs.shape[2]) + depth * rhs.shape[2]),
            transcendentals=0,
        ),
    )(meta, tiles, rhs)
    return [outs[2 * n : 2 * n + 2] for n in range(HALVES)]


def update_kernel(places, has_base, table_ref, meta_ref, mine_ref, theirs_ref, *refs):
    ends = 2 * has_base + STREAMS * len(places)
    sources, scratch = refs[2 * has_base : ends], refs[ends:]
    out_ref, total, part, rows_both, pieces, sem, piece_sem = scratch[:7]
    per, rows = sources[0].shape[:2]
    z, side, last = meta_ref[0], meta_ref[1], meta_ref[2]
    core = (1 - side) // 2
    upstream = jnp.where(core == 0, z, last - z)
    height = part.shape[0] // 2
    blocks = 2 * height // BLOCK
    half = rows // 2
    raw = len(mine_ref.shape) == 3
    only = places[0] if len(places) == 1 else None
    reach = upstream >= places[0]
    if has_base:
        base = pltpu.make_async_copy(refs[0], scratch[7], scratch[8])
        base.start()
        after_ref, next_rows, next_sem = refs[1], scratch[9], scratch[10]
        extend = upstream == places[0]
        nexts = [pltpu.make_async_copy(after_ref.at[s], next_rows.at[s], next_sem.at[s]) for s in range(SNODES)]
    reads, arrive = [], []
    for s in range(SNODES):
        for i, ref in enumerate((mine_ref, theirs_ref)):
            chip = jnp.clip(z - side * places[0], 0, last)
            if only is not None and raw:
                source = ref.at[s, :, pl.ds(pl.multiple_of(chip * rows, rows), rows)]
                spot = rows_both.at[s, pl.ds(i * height, height), pl.ds(0, rows)]
            elif raw:
                source, spot = ref.at[s], rows_both.at[s, pl.ds(i * height, height)]
            else:
                source, spot = ref.at[s], rows_both.at[s, :, pl.ds(i * height, height)]
            reads.append(pltpu.make_async_copy(source, spot, sem.at[s, i]))
            pl.when(reach)(reads[-1].start)
        if has_base:
            pl.when(extend)(nexts[s].start)
        if s % per == 0:
            for i, t in enumerate(places):
                k = (s // per) * len(places) + i
                arrive.append(pltpu.make_async_copy(sources[k], pieces.at[k], piece_sem.at[k]))
                pl.when(upstream >= t)(arrive[-1].start)

    def factor(s, start, count):
        if only is not None and raw:
            return rows_both[s, :, :rows]
        if raw:
            return rows_both[s, :, pl.ds(pl.multiple_of(start * count, count), count)]
        both = rows_both[s, start // (rows // count)]
        return both if count == rows else jnp.where(core == 0, both[:, :count], both[:, count:])

    if has_base:
        base.wait()
        total[...] = scratch[7][...].astype(F32)
    else:
        total[...] = jnp.zeros_like(total)

    @pl.when(reach)
    def _():
        for s in range(SNODES):
            reads[2 * s].wait()
            reads[2 * s + 1].wait()
            first = (s // per) * len(places)
            if s % per == 0:
                for i, t in enumerate(places):
                    pl.when(upstream >= t)(arrive[first + i].wait)
            for i, t in enumerate(places):
                if t == 0:
                    part[...] = jnp.dot(
                        factor(s, 2 * z + core, half),
                        pieces[first, s % per, pl.ds(pl.multiple_of(core * half, half), half)],
                        preferred_element_type=F32,
                    )
                    continue
                chip = jnp.clip(z - side * t, 0, last)
                if i == 0:
                    part[...] = jnp.dot(
                        factor(s, chip, rows), pieces[first, s % per], preferred_element_type=F32
                    )
                    continue

                @pl.when(upstream >= t)
                def _():
                    part[...] += jnp.dot(
                        factor(s, chip, rows), pieces[first + i, s % per], preferred_element_type=F32
                    )

            for b in range(blocks):
                total[table_ref[s * blocks + b]] += part[b * BLOCK : (b + 1) * BLOCK]
            if has_base:

                @pl.when(extend)
                def _():
                    nexts[s].wait()
                    part[...] = jnp.dot(next_rows[s], pieces[first, s % per], preferred_element_type=F32)
                    for b in range(blocks):
                        total[table_ref[(SNODES + s) * blocks + b]] += part[b * BLOCK : (b + 1) * BLOCK]

    out_ref[...] = total[...].astype(out_ref.dtype)


def apply_update(table, meta, mine, theirs, got, places, anc_blocks, *extra):
    pieces = [x[t] for x in got for t in places]
    width = pieces[0].shape[-1]
    height = mine.shape[-2]
    hbm = pl.BlockSpec(memory_space=pl.ANY)
    both = list(mine.shape)
    both[-2] *= 2
    if mine.ndim == 3 and len(places) == 1:
        both[-1] = pieces[0].shape[-2]
    block = (anc_blocks, BLOCK, width)
    has_base = len(extra) // 2
    return pl.pallas_call(
        functools.partial(update_kernel, places, has_base),
        out_shape=jax.ShapeDtypeStruct(block, BF16),
        in_specs=[pl.BlockSpec(memory_space=pltpu.SMEM)] * 2 + [hbm] * (2 + len(extra) + len(pieces)),
        out_specs=pl.BlockSpec(memory_space=pltpu.VMEM),
        scratch_shapes=[
            pltpu.VMEM(block, F32),
            pltpu.VMEM((2 * height, width), F32),
            pltpu.VMEM(tuple(both), BF16),
            pltpu.VMEM((len(pieces),) + pieces[0].shape, BF16),
            pltpu.SemaphoreType.DMA((SNODES, 2)),
            pltpu.SemaphoreType.DMA((len(pieces),)),
        ]
        + [
            pltpu.VMEM(block, BF16),
            pltpu.SemaphoreType.DMA,
            pltpu.VMEM((SNODES, 2 * height, pieces[0].shape[-2]), BF16),
            pltpu.SemaphoreType.DMA((SNODES,)),
        ]
        * has_base,
        compiler_params=pltpu.CompilerParams(vmem_limit_bytes=60 * 1024 * 1024),
        cost_estimate=pl.CostEstimate(
            flops=4 * mine.size * width * len(places) // 4,
            bytes_accessed=mine.size * 4 + anc_blocks * BLOCK * width * 2,
            transcendentals=0,
        ),
    )(table, meta, mine, theirs, *extra, *pieces)


def per_device(inv_diag, off_diag, rhs, anc_rhs, dest_device, dest_slot):
    n_row, n_col = lax.axis_size("row"), lax.axis_size("col")
    nz = n_row // 2
    row, col = lax.axis_index("row"), lax.axis_index("col")
    z, core = row // 2, row % 2
    side = 1 - 2 * core
    own_rows = inv_diag.shape[1] // n_row
    anc_dev = anc_rhs.shape[0] // BLOCK
    anc_blocks = n_row * anc_dev
    width = rhs.shape[2] // HALVES
    per = SNODES // STREAMS
    pair = [(r, r ^ 1) for r in range(n_row)]

    def hop(value, sources):
        up = [(2 * i, 2 * i + 2) for i in sources if i + 1 < nz]
        down = [(2 * (nz - 1 - i) + 1, 2 * (nz - 2 - i) + 1) for i in sources if i + 1 < nz]
        return lax.ppermute(value, "row", up + down)

    tiles = inv_diag.reshape(SNODES, nz, 2 * own_rows, inv_diag.shape[2])
    meta = jnp.stack([z, side, jnp.full_like(z, nz - 1)]).astype(jnp.int32)

    def sum_cores(terms):
        away, keep = terms
        other = lax.ppermute(away, "row", pair)
        return [(keep[0],)] + [(keep[j], other[j - 1]) for j in range(1, nz)]

    turns = [[(i, i ^ d) for i in range(n_col)] for d in range(1, n_col)]
    moves = [[(2 * i + q, 2 * ((i + d) % nz) + q) for i in range(nz) for q in range(2)] for d in range(1, nz)]

    def share_cores(total):
        total = total.reshape(nz, 2, anc_dev, n_col, BLOCK // n_col, width)
        return add16(pick(total, core, 1), lax.ppermute(pick(total, 1 - core, 1), "row", pair))

    def share_col(total):
        return add16(
            pick(total, col, 2),
            *[lax.ppermute(pick(total, col ^ d, 2), "col", turns[d - 1]) for d in range(1, n_col)],
        )

    def share_line(total):
        return add16(
            pick(total, z, 0),
            *[lax.ppermute(pick(total, (z + d) % nz, 0), "row", moves[d - 1]) for d in range(1, nz)],
        )

    def share_out(total):
        whole = jnp.zeros((anc_dev, n_col) + total.shape[1:], BF16)
        whole = lax.dynamic_update_index_in_dim(whole, total, col, 1)
        for d in range(1, n_col):
            other = lax.ppermute(total, "col", turns[d - 1])
            whole = lax.dynamic_update_index_in_dim(whole, other, col ^ d, 1)
        return whole.reshape(anc_dev * BLOCK, whole.shape[-1])

    shares = [share_cores, share_col, share_line]

    per_dev = off_diag.shape[1] // BLOCK
    target = (dest_device[:, :, 0] * anc_dev + dest_slot).reshape(n_row, per_dev, SNODES)
    onward = jnp.clip(row + 2 * side, 0, n_row - 1)
    table = jnp.concatenate(
        [
            jnp.concatenate([pick(target, r, 0), pick(target, r ^ 1, 0)], axis=0).T.reshape(-1)
            for r in (row, onward)
        ]
    )
    split = (lambda x: x) if (own_rows % 128 == 0) else (
        lambda x: x.reshape(SNODES, x.shape[1], nz, 2 * own_rows).transpose(0, 2, 1, 3)
    )

    terms, last = [], ()
    for s in range(STREAMS):
        raw = apply_product(after(meta, *last), tiles, rhs, s * per, per)
        last = (raw[0][1],)
        terms.append([sum_cores(x) for x in raw])

    own = [[None] * HALVES for _ in range(STREAMS)]
    upstream = jnp.where(core == 0, z, nz - 1 - z)
    flows = [()] * STREAMS
    for t in range(1, nz):
        for s in range(STREAMS):
            flows[s] = (hop(add16(*terms[s][0][nz - t], *flows[s]), range(t)),)
        if t == 1:
            theirs = lax.ppermute(after(off_diag, flows[0][0]), "row", pair)
    mine, theirs = split(off_diag), split(theirs)

    waiting = None
    for n in range(HALVES):
        partial = [add16(*terms[s][n][0], *flows[s]) for s in range(STREAMS)]
        for s in range(STREAMS):
            own[s][n] = add16(partial[s], lax.ppermute(partial[s], "row", pair))
        got = [[own[s][n]] for s in range(STREAMS)]
        for t in range(1, nz + 1):
            for s in range(STREAMS):
                send = got[s][-1]
                if n + 1 < HALVES:
                    if t > 1:
                        late = functools.reduce(
                            lambda a, b: a + b, [x.astype(F32) for x in terms[s][n + 1][nz - t + 1]]
                        )
                        send = (send.astype(F32) + jnp.where(upstream >= t - 1, 0.0, late)).astype(BF16)
                    got[s].append(hop(send, range(nz)))
                elif t < nz - 1:
                    got[s].append(hop(send, range(t - 1, nz)))
                    if n and s == 0 and t == 1:
                        total = apply_update(
                            table, after(meta, got[0][1]), mine, theirs, before, range(nz), anc_blocks
                        )
        if n + 1 < HALVES:
            flows = [(got[s].pop(),) for s in range(STREAMS)]
        if n:
            waiting = share_col(share_cores(total))
        before = got
    if mine.ndim == 3:
        last_rows = [lax.dynamic_slice_in_dim(x, core * (nz - 1) * 2 * own_rows, 2 * own_rows, 2) for x in (mine, theirs)]
    else:
        last_rows = [pick(x, core * (nz - 1), 1) for x in (mine, theirs)]
    back = lax.ppermute(
        after(jnp.concatenate(last_rows, axis=1), got[0][1]), "row", [(2 * nz - 2, 2 * nz - 4), (1, 3)]
    )
    total = apply_update(table, after(meta, got[0][nz - 2]), mine, theirs, got, range(nz - 2), anc_blocks)
    total = apply_update(table, after(meta, waiting), mine, theirs, got, [nz - 2], anc_blocks, total, back)
    total = jnp.concatenate([waiting, share_col(share_cores(total))], axis=-1)
    update = share_out(share_line(total))
    solution = jnp.concatenate(
        [jnp.concatenate(
                [lax.dynamic_slice_in_dim(own[s][n], core * own_rows, own_rows, 1) for n in range(HALVES)], axis=2
            ) for s in range(STREAMS)],
        axis=0,
    )
    anc_out = anc_rhs - update.astype(F32)
    return (solution, anc_out)


def solution(mesh):
    in_specs = (
        P(None, "col", "row"),
        P(None, "row", "col"),
        P(None, "row", None),
        P("row", None),
        P(),
        P(),
    )
    out_specs = (P(None, ("col", "row"), None), P("row", None))
    return jax.shard_map(
        per_device, mesh=mesh, in_specs=in_specs, out_specs=out_specs, check_vma=False
    )
```

```python
import functools

import jax
import jax.numpy as jnp
from jax import lax
from jax.experimental import pallas as pl
from jax.experimental.pallas import tpu as pltpu
from jax.sharding import PartitionSpec as P

SNODES = 4
BLOCK = 32
HALVES = 2
AHEAD = 4
STREAMS = 2
F32 = jnp.float32
BF16 = jnp.bfloat16


def add16(*terms):
    return functools.reduce(lambda a, b: a + b, [t.astype(F32) for t in terms]).astype(BF16)


def pick(array, index, axis):
    return lax.dynamic_index_in_dim(array, index, axis, keepdims=False)


def after(value, *earlier):
    return lax.optimization_barrier((value,) + earlier)[0]


def product_kernel(first, meta_ref, tile_ref, rhs_ref, *refs):
    outs, (tile, part, terms, tile_sem, part_sem, out_sem) = refs[:-6], refs[-6:]
    per, nz = tile.shape[:2]
    z, side = meta_ref[0], meta_ref[1]
    width = terms.shape[-1]
    reads = []
    for s in range(per):
        reads.append([pltpu.make_async_copy(rhs_ref.at[first + s], part.at[s], part_sem.at[s])])
        for d in range(nz):
            reads[s].append(pltpu.make_async_copy(tile_ref.at[first + s, d], tile.at[s, d], tile_sem.at[s, d]))
    queue = [copy for copies in reads for copy in copies]
    for copy in queue[:AHEAD]:
        copy.start()
    queue = queue[AHEAD:]

    def await_next(copy):
        copy.wait()
        if queue:
            queue.pop(0).start()

    writes = []
    for s in range(per):
        await_next(reads[s][0])
        for d in range(nz):
            await_next(reads[s][d + 1])
            both = jnp.dot(tile[s, d], part[s], preferred_element_type=F32).astype(BF16)
            place = (d - z) * side
            for n in range(HALVES):
                terms[s, d, n] = both[:, n * width : (n + 1) * width]
                source, sem = terms.at[s, d, n], out_sem.at[s, d, n]
                away = pltpu.make_async_copy(source, outs[2 * n].at[jnp.clip(-1 - place, 0, nz - 2), s], sem)
                keep = pltpu.make_async_copy(source, outs[2 * n + 1].at[jnp.clip(place, 0, nz - 1), s], sem)
                pl.when(place < 0)(away.start)
                pl.when(place >= 0)(keep.start)
                writes.append((place, away, keep))
    for place, away, keep in writes:
        pl.when(place < 0)(away.wait)
        pl.when(place >= 0)(keep.wait)


def apply_product(meta, tiles, rhs, first, per):
    nz, rows, depth = tiles.shape[1:]
    width = rhs.shape[2] // HALVES
    hbm = pl.BlockSpec(memory_space=pl.ANY)
    outs = pl.pallas_call(
        functools.partial(product_kernel, first),
        in_specs=[pl.BlockSpec(memory_space=pltpu.SMEM), hbm, hbm],
        out_specs=[hbm] * (2 * HALVES),
        out_shape=[
            jax.ShapeDtypeStruct((nz - 1, per, rows, width), BF16),
            jax.ShapeDtypeStruct((nz, per, rows, width), BF16),
        ]
        * HALVES,
        scratch_shapes=[
            pltpu.VMEM((per, nz, rows, depth), BF16),
            pltpu.VMEM((per, depth, rhs.shape[2]), BF16),
            pltpu.VMEM((per, nz, HALVES, rows, width), BF16),
            pltpu.SemaphoreType.DMA((per, nz)),
            pltpu.SemaphoreType.DMA((per,)),
            pltpu.SemaphoreType.DMA((per, nz, HALVES)),
        ],
        compiler_params=pltpu.CompilerParams(vmem_limit_bytes=56 * 1024 * 1024),
        cost_estimate=pl.CostEstimate(
            flops=2 * per * nz * rows * depth * rhs.shape[2],
            bytes_accessed=2 * per * (nz * rows * (depth + rhs.shape[2]) + depth * rhs.shape[2]),
            transcendentals=0,
        ),
    )(meta, tiles, rhs)
    return [outs[2 * n : 2 * n + 2] for n in range(HALVES)]


def update_kernel(places, has_base, table_ref, meta_ref, mine_ref, theirs_ref, *refs):
    ends = 2 * has_base + STREAMS * len(places)
    sources, scratch = refs[2 * has_base : ends], refs[ends:]
    out_ref, total, part, rows_both, pieces, sem, piece_sem = scratch[:7]
    per, rows = sources[0].shape[:2]
    z, side, last = meta_ref[0], meta_ref[1], meta_ref[2]
    core = (1 - side) // 2
    upstream = jnp.where(core == 0, z, last - z)
    height = part.shape[0] // 2
    blocks = 2 * height // BLOCK
    half = rows // 2
    raw = len(mine_ref.shape) == 3
    only = places[0] if len(places) == 1 else None
    reach = upstream >= places[0]
    if has_base:
        base = pltpu.make_async_copy(refs[0], scratch[7], scratch[8])
        base.start()
        after_ref, next_rows, next_sem = refs[1], scratch[9], scratch[10]
        extend = upstream == places[0]
        nexts = [pltpu.make_async_copy(after_ref.at[s], next_rows.at[s], next_sem.at[s]) for s in range(SNODES)]
    reads, arrive = [], []
    for s in range(SNODES):
        for i, ref in enumerate((mine_ref, theirs_ref)):
            chip = jnp.clip(z - side * places[0], 0, last)
            if only is not None and raw:
                source = ref.at[s, :, pl.ds(pl.multiple_of(chip * rows, rows), rows)]
                spot = rows_both.at[s, pl.ds(i * height, height), pl.ds(0, rows)]
            elif raw:
                source, spot = ref.at[s], rows_both.at[s, pl.ds(i * height, height)]
            else:
                source, spot = ref.at[s], rows_both.at[s, :, pl.ds(i * height, height)]
            reads.append(pltpu.make_async_copy(source, spot, sem.at[s, i]))
        if s % per == 0:
            for i, t in enumerate(places):
                k = (s // per) * len(places) + i
                arrive.append(pltpu.make_async_copy(sources[k], pieces.at[k], piece_sem.at[k]))

    def begin(s):
        for read in reads[2 * s : 2 * s + 2]:
            pl.when(reach)(read.start)
        if has_base:
            pl.when(extend)(nexts[s].start)
        if s % per == 0:
            for i, t in enumerate(places):
                pl.when(upstream >= t)(arrive[(s // per) * len(places) + i].start)

    begin(0)
    begin(1)

    def factor(s, start, count):
        if only is not None and raw:
            return rows_both[s, :, :rows]
        if raw:
            return rows_both[s, :, pl.ds(pl.multiple_of(start * count, count), count)]
        both = rows_both[s, start // (rows // count)]
        return both if count == rows else jnp.where(core == 0, both[:, :count], both[:, count:])

    if has_base:
        base.wait()
        total[...] = scratch[7][...].astype(F32)
    else:
        total[...] = jnp.zeros_like(total)

    @pl.when(reach)
    def _():
        for s in range(SNODES):
            reads[2 * s].wait()
            reads[2 * s + 1].wait()
            first = (s // per) * len(places)
            if s % per == 0:
                for i, t in enumerate(places):
                    pl.when(upstream >= t)(arrive[first + i].wait)
            if s + 2 < SNODES:
                begin(s + 2)
            for i, t in enumerate(places):
                if t == 0:
                    part[...] = jnp.dot(
                        factor(s, 2 * z + core, half),
                        pieces[first, s % per, pl.ds(pl.multiple_of(core * half, half), half)],
                        preferred_element_type=F32,
                    )
                    continue
                chip = jnp.clip(z - side * t, 0, last)
                if i == 0:
                    part[...] = jnp.dot(
                        factor(s, chip, rows), pieces[first, s % per], preferred_element_type=F32
                    )
                    continue

                @pl.when(upstream >= t)
                def _():
                    part[...] += jnp.dot(
                        factor(s, chip, rows), pieces[first + i, s % per], preferred_element_type=F32
                    )

            for b in range(blocks):
                total[table_ref[s * blocks + b]] += part[b * BLOCK : (b + 1) * BLOCK]
            if has_base:

                @pl.when(extend)
                def _():
                    nexts[s].wait()
                    part[...] = jnp.dot(next_rows[s], pieces[first, s % per], preferred_element_type=F32)
                    for b in range(blocks):
                        total[table_ref[(SNODES + s) * blocks + b]] += part[b * BLOCK : (b + 1) * BLOCK]

    out_ref[...] = total[...].astype(out_ref.dtype)


def apply_update(table, meta, mine, theirs, got, places, anc_blocks, *extra):
    pieces = [x[t] for x in got for t in places]
    width = pieces[0].shape[-1]
    height = mine.shape[-2]
    hbm = pl.BlockSpec(memory_space=pl.ANY)
    both = list(mine.shape)
    both[-2] *= 2
    if mine.ndim == 3 and len(places) == 1:
        both[-1] = pieces[0].shape[-2]
    block = (anc_blocks, BLOCK, width)
    has_base = len(extra) // 2
    return pl.pallas_call(
        functools.partial(update_kernel, places, has_base),
        out_shape=jax.ShapeDtypeStruct(block, BF16),
        in_specs=[pl.BlockSpec(memory_space=pltpu.SMEM)] * 2 + [hbm] * (2 + len(extra) + len(pieces)),
        out_specs=pl.BlockSpec(memory_space=pltpu.VMEM),
        scratch_shapes=[
            pltpu.VMEM(block, F32),
            pltpu.VMEM((2 * height, width), F32),
            pltpu.VMEM(tuple(both), BF16),
            pltpu.VMEM((len(pieces),) + pieces[0].shape, BF16),
            pltpu.SemaphoreType.DMA((SNODES, 2)),
            pltpu.SemaphoreType.DMA((len(pieces),)),
        ]
        + [
            pltpu.VMEM(block, BF16),
            pltpu.SemaphoreType.DMA,
            pltpu.VMEM((SNODES, 2 * height, pieces[0].shape[-2]), BF16),
            pltpu.SemaphoreType.DMA((SNODES,)),
        ]
        * has_base,
        compiler_params=pltpu.CompilerParams(vmem_limit_bytes=60 * 1024 * 1024),
        cost_estimate=pl.CostEstimate(
            flops=4 * mine.size * width * len(places) // 4,
            bytes_accessed=mine.size * 4 + anc_blocks * BLOCK * width * 2,
            transcendentals=0,
        ),
    )(table, meta, mine, theirs, *extra, *pieces)


def per_device(inv_diag, off_diag, rhs, anc_rhs, dest_device, dest_slot):
    n_row, n_col = lax.axis_size("row"), lax.axis_size("col")
    nz = n_row // 2
    row, col = lax.axis_index("row"), lax.axis_index("col")
    z, core = row // 2, row % 2
    side = 1 - 2 * core
    own_rows = inv_diag.shape[1] // n_row
    anc_dev = anc_rhs.shape[0] // BLOCK
    anc_blocks = n_row * anc_dev
    width = rhs.shape[2] // HALVES
    per = SNODES // STREAMS
    pair = [(r, r ^ 1) for r in range(n_row)]

    def hop(value, sources):
        up = [(2 * i, 2 * i + 2) for i in sources if i + 1 < nz]
        down = [(2 * (nz - 1 - i) + 1, 2 * (nz - 2 - i) + 1) for i in sources if i + 1 < nz]
        return lax.ppermute(value, "row", up + down)

    tiles = inv_diag.reshape(SNODES, nz, 2 * own_rows, inv_diag.shape[2])
    meta = jnp.stack([z, side, jnp.full_like(z, nz - 1)]).astype(jnp.int32)

    def sum_cores(terms):
        away, keep = terms
        other = lax.ppermute(away, "row", pair)
        return [(keep[0],)] + [(keep[j], other[j - 1]) for j in range(1, nz)]

    turns = [[(i, i ^ d) for i in range(n_col)] for d in range(1, n_col)]
    moves = [[(2 * i + q, 2 * ((i + d) % nz) + q) for i in range(nz) for q in range(2)] for d in range(1, nz)]

    def share_cores(total):
        total = total.reshape(nz, 2, anc_dev, n_col, BLOCK // n_col, width)
        return add16(pick(total, core, 1), lax.ppermute(pick(total, 1 - core, 1), "row", pair))

    def share_col(total):
        return add16(
            pick(total, col, 2),
            *[lax.ppermute(pick(total, col ^ d, 2), "col", turns[d - 1]) for d in range(1, n_col)],
        )

    def share_line(total):
        return add16(
            pick(total, z, 0),
            *[lax.ppermute(pick(total, (z + d) % nz, 0), "row", moves[d - 1]) for d in range(1, nz)],
        )

    def share_out(total):
        whole = jnp.zeros((anc_dev, n_col) + total.shape[1:], BF16)
        whole = lax.dynamic_update_index_in_dim(whole, total, col, 1)
        for d in range(1, n_col):
            other = lax.ppermute(total, "col", turns[d - 1])
            whole = lax.dynamic_update_index_in_dim(whole, other, col ^ d, 1)
        return whole.reshape(anc_dev * BLOCK, whole.shape[-1])

    shares = [share_cores, share_col, share_line]

    per_dev = off_diag.shape[1] // BLOCK
    target = (dest_device[:, :, 0] * anc_dev + dest_slot).reshape(n_row, per_dev, SNODES)
    onward = jnp.clip(row + 2 * side, 0, n_row - 1)
    table = jnp.concatenate(
        [
            jnp.concatenate([pick(target, r, 0), pick(target, r ^ 1, 0)], axis=0).T.reshape(-1)
            for r in (row, onward)
        ]
    )
    split = (lambda x: x) if (own_rows % 128 == 0) else (
        lambda x: x.reshape(SNODES, x.shape[1], nz, 2 * own_rows).transpose(0, 2, 1, 3)
    )

    terms, last = [], ()
    for s in range(STREAMS):
        raw = apply_product(after(meta, *last), tiles, rhs, s * per, per)
        last = (raw[0][1],)
        terms.append([sum_cores(x) for x in raw])

    own = [[None] * HALVES for _ in range(STREAMS)]
    upstream = jnp.where(core == 0, z, nz - 1 - z)
    flows = [()] * STREAMS
    for t in range(1, nz):
        for s in range(STREAMS):
            flows[s] = (hop(add16(*terms[s][0][nz - t], *flows[s]), range(t)),)
        if t == 1:
            theirs = lax.ppermute(after(off_diag, flows[0][0]), "row", pair)
    mine, theirs = split(off_diag), split(theirs)

    waiting = None
    for n in range(HALVES):
        partial = [add16(*terms[s][n][0], *flows[s]) for s in range(STREAMS)]
        for s in range(STREAMS):
            own[s][n] = add16(partial[s], lax.ppermute(partial[s], "row", pair))
        got = [[own[s][n]] for s in range(STREAMS)]
        for t in range(1, nz + 1):
            for s in range(STREAMS):
                send = got[s][-1]
                if n + 1 < HALVES:
                    if t > 1:
                        late = functools.reduce(
                            lambda a, b: a + b, [x.astype(F32) for x in terms[s][n + 1][nz - t + 1]]
                        )
                        send = (send.astype(F32) + jnp.where(upstream >= t - 1, 0.0, late)).astype(BF16)
                    got[s].append(hop(send, range(nz)))
                elif t < nz - 1:
                    got[s].append(hop(send, range(t - 1, nz)))
                    if n and s == 0 and t == 1:
                        total = apply_update(
                            table, after(meta, got[0][1]), mine, theirs, before, range(nz), anc_blocks
                        )
        if n + 1 < HALVES:
            flows = [(got[s].pop(),) for s in range(STREAMS)]
        if n:
            total = share_cores(total)
            waiting = share_col(total)
        before = got
    if mine.ndim == 3:
        last_rows = [lax.dynamic_slice_in_dim(x, core * (nz - 1) * 2 * own_rows, 2 * own_rows, 2) for x in (mine, theirs)]
    else:
        last_rows = [pick(x, core * (nz - 1), 1) for x in (mine, theirs)]
    back = lax.ppermute(
        after(jnp.concatenate(last_rows, axis=1), got[0][1]), "row", [(2 * nz - 2, 2 * nz - 4), (1, 3)]
    )
    total = apply_update(table, after(meta, total), mine, theirs, got, range(nz - 2), anc_blocks)
    total = apply_update(table, after(meta, waiting), mine, theirs, got, [nz - 2], anc_blocks, total, back)
    total = jnp.concatenate([waiting, share_col(share_cores(total))], axis=-1)
    update = share_out(share_line(total))
    solution = jnp.concatenate(
        [jnp.concatenate(
                [lax.dynamic_slice_in_dim(own[s][n], core * own_rows, own_rows, 1) for n in range(HALVES)], axis=2
            ) for s in range(STREAMS)],
        axis=0,
    )
    anc_out = anc_rhs - update.astype(F32)
    return (solution, anc_out)


def solution(mesh):
    in_specs = (
        P(None, "col", "row"),
        P(None, "row", "col"),
        P(None, "row", None),
        P("row", None),
        P(),
        P(),
    )
    out_specs = (P(None, ("col", "row"), None), P("row", None))
    return jax.shard_map(
        per_device, mesh=mesh, in_specs=in_specs, out_specs=out_specs, check_vma=False
    )
```

```python
import functools

import jax
import jax.numpy as jnp
from jax import lax
from jax.experimental import pallas as pl
from jax.experimental.pallas import tpu as pltpu
from jax.sharding import PartitionSpec as P

SNODES = 4
BLOCK = 32
HALVES = 2
AHEAD = 4
STREAMS = 2
F32 = jnp.float32
BF16 = jnp.bfloat16


def add16(*terms):
    return functools.reduce(lambda a, b: a + b, [t.astype(F32) for t in terms]).astype(BF16)


def pick(array, index, axis):
    return lax.dynamic_index_in_dim(array, index, axis, keepdims=False)


def after(value, *earlier):
    return lax.optimization_barrier((value,) + earlier)[0]


def product_kernel(first, meta_ref, tile_ref, rhs_ref, *refs):
    outs, (tile, part, terms, tile_sem, part_sem, out_sem) = refs[:-6], refs[-6:]
    per, nz = tile.shape[:2]
    z, side = meta_ref[0], meta_ref[1]
    width = terms.shape[-1]
    reads = []
    for s in range(per):
        reads.append([pltpu.make_async_copy(rhs_ref.at[first + s], part.at[s], part_sem.at[s])])
        for d in range(nz):
            reads[s].append(pltpu.make_async_copy(tile_ref.at[first + s, d], tile.at[s, d], tile_sem.at[s, d]))
    queue = [copy for copies in reads for copy in copies]
    for copy in queue[:AHEAD]:
        copy.start()
    queue = queue[AHEAD:]

    def await_next(copy):
        copy.wait()
        if queue:
            queue.pop(0).start()

    writes = []
    for s in range(per):
        await_next(reads[s][0])
        for d in range(nz):
            await_next(reads[s][d + 1])
            both = jnp.dot(tile[s, d], part[s], preferred_element_type=F32).astype(BF16)
            place = (d - z) * side
            for n in range(HALVES):
                terms[s, d, n] = both[:, n * width : (n + 1) * width]
                source, sem = terms.at[s, d, n], out_sem.at[s, d, n]
                away = pltpu.make_async_copy(source, outs[2 * n].at[jnp.clip(-1 - place, 0, nz - 2), s], sem)
                keep = pltpu.make_async_copy(source, outs[2 * n + 1].at[jnp.clip(place, 0, nz - 1), s], sem)
                pl.when(place < 0)(away.start)
                pl.when(place >= 0)(keep.start)
                writes.append((place, away, keep))
    for place, away, keep in writes:
        pl.when(place < 0)(away.wait)
        pl.when(place >= 0)(keep.wait)


def apply_product(meta, tiles, rhs, first, per):
    nz, rows, depth = tiles.shape[1:]
    width = rhs.shape[2] // HALVES
    hbm = pl.BlockSpec(memory_space=pl.ANY)
    outs = pl.pallas_call(
        functools.partial(product_kernel, first),
        in_specs=[pl.BlockSpec(memory_space=pltpu.SMEM), hbm, hbm],
        out_specs=[hbm] * (2 * HALVES),
        out_shape=[
            jax.ShapeDtypeStruct((nz - 1, per, rows, width), BF16),
            jax.ShapeDtypeStruct((nz, per, rows, width), BF16),
        ]
        * HALVES,
        scratch_shapes=[
            pltpu.VMEM((per, nz, rows, depth), BF16),
            pltpu.VMEM((per, depth, rhs.shape[2]), BF16),
            pltpu.VMEM((per, nz, HALVES, rows, width), BF16),
            pltpu.SemaphoreType.DMA((per, nz)),
            pltpu.SemaphoreType.DMA((per,)),
            pltpu.SemaphoreType.DMA((per, nz, HALVES)),
        ],
        compiler_params=pltpu.CompilerParams(vmem_limit_bytes=56 * 1024 * 1024),
        cost_estimate=pl.CostEstimate(
            flops=2 * per * nz * rows * depth * rhs.shape[2],
            bytes_accessed=2 * per * (nz * rows * (depth + rhs.shape[2]) + depth * rhs.shape[2]),
            transcendentals=0,
        ),
    )(meta, tiles, rhs)
    return [outs[2 * n : 2 * n + 2] for n in range(HALVES)]


def update_kernel(places, has_base, table_ref, meta_ref, mine_ref, theirs_ref, *refs):
    ends = 2 * has_base + STREAMS * len(places)
    sources, scratch = refs[2 * has_base : ends], refs[ends:]
    out_ref, total, part, rows_both, pieces, sem, piece_sem = scratch[:7]
    per, rows = sources[0].shape[:2]
    z, side, last = meta_ref[0], meta_ref[1], meta_ref[2]
    core = (1 - side) // 2
    upstream = jnp.where(core == 0, z, last - z)
    height = part.shape[0] // 2
    blocks = 2 * height // BLOCK
    half = rows // 2
    raw = len(mine_ref.shape) == 3
    only = places[0] if len(places) == 1 else None
    reach = upstream >= places[0]
    if has_base:
        base = pltpu.make_async_copy(refs[0], scratch[7], scratch[8])
        base.start()
        after_ref, next_rows, next_sem = refs[1], scratch[9], scratch[10]
        extend = upstream == places[0]
        nexts = [pltpu.make_async_copy(after_ref.at[s], next_rows.at[s], next_sem.at[s]) for s in range(SNODES)]
    reads, arrive = [], []
    for s in range(SNODES):
        for i, ref in enumerate((mine_ref, theirs_ref)):
            chip = jnp.clip(z - side * places[0], 0, last)
            if only is not None and raw:
                source = ref.at[s, :, pl.ds(pl.multiple_of(chip * rows, rows), rows)]
                spot = rows_both.at[s, pl.ds(i * height, height), pl.ds(0, rows)]
            elif raw:
                source, spot = ref.at[s], rows_both.at[s, pl.ds(i * height, height)]
            else:
                source, spot = ref.at[s], rows_both.at[s, :, pl.ds(i * height, height)]
            reads.append(pltpu.make_async_copy(source, spot, sem.at[s, i]))
        if s % per == 0:
            for i, t in enumerate(places):
                k = (s // per) * len(places) + i
                arrive.append(pltpu.make_async_copy(sources[k], pieces.at[k], piece_sem.at[k]))

    def begin(s):
        for read in reads[2 * s : 2 * s + 2]:
            pl.when(reach)(read.start)
        if has_base:
            pl.when(extend)(nexts[s].start)
        if s % per == 0:
            for i, t in enumerate(places):
                pl.when(upstream >= t)(arrive[(s // per) * len(places) + i].start)

    begin(0)
    begin(1)

    def factor(s, start, count):
        if only is not None and raw:
            return rows_both[s, :, :rows]
        if raw:
            return rows_both[s, :, pl.ds(pl.multiple_of(start * count, count), count)]
        both = rows_both[s, start // (rows // count)]
        return both if count == rows else jnp.where(core == 0, both[:, :count], both[:, count:])

    if has_base:
        base.wait()
        total[...] = scratch[7][...].astype(F32)
    else:
        total[...] = jnp.zeros_like(total)

    @pl.when(reach)
    def _():
        for s in range(SNODES):
            reads[2 * s].wait()
            reads[2 * s + 1].wait()
            first = (s // per) * len(places)
            if s % per == 0:
                for i, t in enumerate(places):
                    pl.when(upstream >= t)(arrive[first + i].wait)
            if s + 2 < SNODES:
                begin(s + 2)
            for i, t in enumerate(places):
                if t == 0:
                    part[...] = jnp.dot(
                        factor(s, 2 * z + core, half),
                        pieces[first, s % per, pl.ds(pl.multiple_of(core * half, half), half)],
                        preferred_element_type=F32,
                    )
                    continue
                chip = jnp.clip(z - side * t, 0, last)
                if i == 0:

                    @pl.when(jnp.logical_not(extend))
                    def _():
                        part[...] = jnp.dot(
                            factor(s, chip, rows), pieces[first, s % per], preferred_element_type=F32
                        )

                    continue

                @pl.when(upstream >= t)
                def _():
                    part[...] += jnp.dot(
                        factor(s, chip, rows), pieces[first + i, s % per], preferred_element_type=F32
                    )

            if has_base:

                @pl.when(extend)
                def _():
                    nexts[s].wait()
                    chip = jnp.clip(z - side * places[0], 0, last)
                    rows_all = jnp.concatenate([factor(s, chip, rows), next_rows[s]], axis=0)
                    tall = jnp.dot(rows_all, pieces[first, s % per], preferred_element_type=F32)
                    part[...] = tall[: blocks * BLOCK]
                    for b in range(blocks):
                        total[table_ref[(SNODES + s) * blocks + b]] += tall[
                            (blocks + b) * BLOCK : (blocks + b + 1) * BLOCK
                        ]

            for b in range(blocks):
                total[table_ref[s * blocks + b]] += part[b * BLOCK : (b + 1) * BLOCK]

    out_ref[...] = total[...].astype(out_ref.dtype)


def apply_update(table, meta, mine, theirs, got, places, anc_blocks, *extra):
    pieces = [x[t] for x in got for t in places]
    width = pieces[0].shape[-1]
    height = mine.shape[-2]
    hbm = pl.BlockSpec(memory_space=pl.ANY)
    both = list(mine.shape)
    both[-2] *= 2
    if mine.ndim == 3 and len(places) == 1:
        both[-1] = pieces[0].shape[-2]
    block = (anc_blocks, BLOCK, width)
    has_base = len(extra) // 2
    return pl.pallas_call(
        functools.partial(update_kernel, places, has_base),
        out_shape=jax.ShapeDtypeStruct(block, BF16),
        in_specs=[pl.BlockSpec(memory_space=pltpu.SMEM)] * 2 + [hbm] * (2 + len(extra) + len(pieces)),
        out_specs=pl.BlockSpec(memory_space=pltpu.VMEM),
        scratch_shapes=[
            pltpu.VMEM(block, F32),
            pltpu.VMEM((2 * height, width), F32),
            pltpu.VMEM(tuple(both), BF16),
            pltpu.VMEM((len(pieces),) + pieces[0].shape, BF16),
            pltpu.SemaphoreType.DMA((SNODES, 2)),
            pltpu.SemaphoreType.DMA((len(pieces),)),
        ]
        + [
            pltpu.VMEM(block, BF16),
            pltpu.SemaphoreType.DMA,
            pltpu.VMEM((SNODES, 2 * height, pieces[0].shape[-2]), BF16),
            pltpu.SemaphoreType.DMA((SNODES,)),
        ]
        * has_base,
        compiler_params=pltpu.CompilerParams(vmem_limit_bytes=60 * 1024 * 1024),
        cost_estimate=pl.CostEstimate(
            flops=4 * mine.size * width * len(places) // 4,
            bytes_accessed=mine.size * 4 + anc_blocks * BLOCK * width * 2,
            transcendentals=0,
        ),
    )(table, meta, mine, theirs, *extra, *pieces)


def per_device(inv_diag, off_diag, rhs, anc_rhs, dest_device, dest_slot):
    n_row, n_col = lax.axis_size("row"), lax.axis_size("col")
    nz = n_row // 2
    row, col = lax.axis_index("row"), lax.axis_index("col")
    z, core = row // 2, row % 2
    side = 1 - 2 * core
    own_rows = inv_diag.shape[1] // n_row
    anc_dev = anc_rhs.shape[0] // BLOCK
    anc_blocks = n_row * anc_dev
    width = rhs.shape[2] // HALVES
    per = SNODES // STREAMS
    pair = [(r, r ^ 1) for r in range(n_row)]

    def hop(value, sources):
        up = [(2 * i, 2 * i + 2) for i in sources if i + 1 < nz]
        down = [(2 * (nz - 1 - i) + 1, 2 * (nz - 2 - i) + 1) for i in sources if i + 1 < nz]
        return lax.ppermute(value, "row", up + down)

    tiles = inv_diag.reshape(SNODES, nz, 2 * own_rows, inv_diag.shape[2])
    meta = jnp.stack([z, side, jnp.full_like(z, nz - 1)]).astype(jnp.int32)

    def sum_cores(terms):
        away, keep = terms
        other = lax.ppermute(away, "row", pair)
        return [(keep[0],)] + [(keep[j], other[j - 1]) for j in range(1, nz)]

    turns = [[(i, i ^ d) for i in range(n_col)] for d in range(1, n_col)]
    moves = [[(2 * i + q, 2 * ((i + d) % nz) + q) for i in range(nz) for q in range(2)] for d in range(1, nz)]

    def share_cores(total):
        total = total.reshape(nz, 2, anc_dev, n_col, BLOCK // n_col, width)
        return add16(pick(total, core, 1), lax.ppermute(pick(total, 1 - core, 1), "row", pair))

    def share_col(total):
        return add16(
            pick(total, col, 2),
            *[lax.ppermute(pick(total, col ^ d, 2), "col", turns[d - 1]) for d in range(1, n_col)],
        )

    def share_line(total):
        return add16(
            pick(total, z, 0),
            *[lax.ppermute(pick(total, (z + d) % nz, 0), "row", moves[d - 1]) for d in range(1, nz)],
        )

    def share_out(total):
        whole = jnp.zeros((anc_dev, n_col) + total.shape[1:], BF16)
        whole = lax.dynamic_update_index_in_dim(whole, total, col, 1)
        for d in range(1, n_col):
            other = lax.ppermute(total, "col", turns[d - 1])
            whole = lax.dynamic_update_index_in_dim(whole, other, col ^ d, 1)
        return whole.reshape(anc_dev * BLOCK, whole.shape[-1])

    shares = [share_cores, share_col, share_line]

    per_dev = off_diag.shape[1] // BLOCK
    target = (dest_device[:, :, 0] * anc_dev + dest_slot).reshape(n_row, per_dev, SNODES)
    onward = jnp.clip(row + 2 * side, 0, n_row - 1)
    table = jnp.concatenate(
        [
            jnp.concatenate([pick(target, r, 0), pick(target, r ^ 1, 0)], axis=0).T.reshape(-1)
            for r in (row, onward)
        ]
    )
    split = (lambda x: x) if (own_rows % 128 == 0) else (
        lambda x: x.reshape(SNODES, x.shape[1], nz, 2 * own_rows).transpose(0, 2, 1, 3)
    )

    terms, last = [], ()
    for s in range(STREAMS):
        raw = apply_product(after(meta, *last), tiles, rhs, s * per, per)
        last = (raw[0][1],)
        terms.append([sum_cores(x) for x in raw])

    own = [[None] * HALVES for _ in range(STREAMS)]
    upstream = jnp.where(core == 0, z, nz - 1 - z)
    flows = [()] * STREAMS
    for t in range(1, nz):
        for s in range(STREAMS):
            flows[s] = (hop(add16(*terms[s][0][nz - t], *flows[s]), range(t)),)
        if t == 1:
            theirs = lax.ppermute(after(off_diag, flows[0][0]), "row", pair)
    mine, theirs = split(off_diag), split(theirs)

    waiting = None
    for n in range(HALVES):
        partial = [add16(*terms[s][n][0], *flows[s]) for s in range(STREAMS)]
        for s in range(STREAMS):
            own[s][n] = add16(partial[s], lax.ppermute(partial[s], "row", pair))
        got = [[own[s][n]] for s in range(STREAMS)]
        for t in range(1, nz + 1):
            for s in range(STREAMS):
                send = got[s][-1]
                if n + 1 < HALVES:
                    if t > 1:
                        late = functools.reduce(
                            lambda a, b: a + b, [x.astype(F32) for x in terms[s][n + 1][nz - t + 1]]
                        )
                        send = (send.astype(F32) + jnp.where(upstream >= t - 1, 0.0, late)).astype(BF16)
                    got[s].append(hop(send, range(nz)))
                elif t < nz - 1:
                    got[s].append(hop(send, range(t - 1, nz)))
                    if n and s == 0 and t == 1:
                        total = apply_update(
                            table, after(meta, got[0][1]), mine, theirs, before, range(nz), anc_blocks
                        )
        if n + 1 < HALVES:
            flows = [(got[s].pop(),) for s in range(STREAMS)]
        if n:
            total = share_cores(total)
            waiting = share_col(total)
        before = got
    if mine.ndim == 3:
        last_rows = [lax.dynamic_slice_in_dim(x, core * (nz - 1) * 2 * own_rows, 2 * own_rows, 2) for x in (mine, theirs)]
    else:
        last_rows = [pick(x, core * (nz - 1), 1) for x in (mine, theirs)]
    back = lax.ppermute(
        after(jnp.concatenate(last_rows, axis=1), got[0][1]), "row", [(2 * nz - 2, 2 * nz - 4), (1, 3)]
    )
    total = apply_update(table, after(meta, total), mine, theirs, got, range(nz - 2), anc_blocks)
    total = apply_update(table, after(meta, waiting), mine, theirs, got, [nz - 2], anc_blocks, total, back)
    total = jnp.concatenate([waiting, share_col(share_cores(total))], axis=-1)
    update = share_out(share_line(total))
    solution = jnp.concatenate(
        [jnp.concatenate(
                [lax.dynamic_slice_in_dim(own[s][n], core * own_rows, own_rows, 1) for n in range(HALVES)], axis=2
            ) for s in range(STREAMS)],
        axis=0,
    )
    anc_out = anc_rhs - update.astype(F32)
    return (solution, anc_out)


def solution(mesh):
    in_specs = (
        P(None, "col", "row"),
        P(None, "row", "col"),
        P(None, "row", None),
        P("row", None),
        P(),
        P(),
    )
    out_specs = (P(None, ("col", "row"), None), P("row", None))
    return jax.shard_map(
        per_device, mesh=mesh, in_specs=in_specs, out_specs=out_specs, check_vma=False
    )
```
